32 devices in a mesh: dp: 4 (over y, x), expert: 8 (over z, core).
Axes of the slice: x: 2, y: 2, z: 4, core: 2. Of those that a mesh axis runs over, the one named last changes fastest.
Arguments:
- tokens: bfloat16 [4096, 2048], P(('dp', 'expert')), may hold values from -6 to 6
- cotangent: bfloat16 [4096, 2048], P(('dp', 'expert')), may hold values from -6 to 6
- routes: int32 [4096, 2], P(('dp', 'expert')), may hold values from 0 to 7, as said below
- route_weights: float32 [4096, 2], P(('dp', 'expert')), may hold values from 0.1 to 1
- capacity: int32 [8], replicated, may hold values from 16 to 32, as said below
- w_in: bfloat16 [8, 2, 1408, 2048], P('expert', None, 'dp'), may hold values from -0.125 to 0.125
- w_down: bfloat16 [8, 1408, 2048], P('expert', 'dp'), may hold values from -0.15625 to 0.15625
Outputs:
- mixed: bfloat16 [4096, 2048], P(('dp', 'expert'))
- d_tokens: bfloat16 [4096, 2048], P(('dp', 'expert'))
- d_route_weights: float32 [4096, 2], P(('dp', 'expert'))
- d_w_in: bfloat16 [8, 2, 1408, 2048], P('expert', None, 'dp')
- d_w_down: bfloat16 [8, 1408, 2048], P('expert', 'dp')
The draws below stay inside these ranges and needn't reach their ends.
Inputs may be any that keep to these rules, and one draw needn't show every extreme that they name: Each token names two different experts; in every block of 128 rows (one device's tokens) some expert whose capacity is 32 is named by 32 or more routes. Some expert has capacity 32.
All inputs are finite; a program needn't handle non-finite values.
Results may differ from the reference program's by a relative error of at most 0.013.
Values may be sent and summed in bfloat16 or wider, within the bound.
A program may use at most 128 MiB of HBM per device.

```python
import jax
import jax.numpy as jnp
from jax import lax

D = 2048
FF = 1408
TOK_DEV = 128
EXPERTS = 8
TOKENS = 4096
CAP = 32


def pick_full(key):
    return jax.random.randint(jax.random.fold_in(key, 7), (), 0, EXPERTS)


def draw_capacity(key, part):
    full_expert = pick_full(key)
    lowest = max(1, CAP // 2)
    values = jax.random.randint(jax.random.fold_in(key, 11), (EXPERTS,), lowest, CAP + 1)
    expert_ids = jnp.arange(EXPERTS)
    return jnp.where(expert_ids == full_expert, CAP, values).astype(jnp.int32)


def draw_routes(key, part):
    num_blocks = TOKENS // TOK_DEV
    full_expert = pick_full(key)
    keys = jax.random.split(jax.random.fold_in(key, 23), 5)
    table = jax.random.permutation(keys[0], EXPERTS)
    first_a = jax.random.randint(keys[1], (TOKENS,), 0, EXPERTS)
    first_b = jax.random.randint(keys[2], (TOKENS,), 0, EXPERTS)
    first = table[jnp.minimum(first_a, first_b)]
    second = (first + 1 + jax.random.randint(keys[3], (TOKENS,), 0, EXPERTS - 1)) % EXPERTS
    offsets = jax.random.randint(keys[4], (num_blocks,), 0, TOK_DEV)
    position = jnp.arange(TOKENS) % TOK_DEV
    block_of = jnp.arange(TOKENS) // TOK_DEV
    forced = (position - offsets[block_of]) % TOK_DEV < CAP
    second = jnp.where(forced & (second == full_expert), (full_expert + 1) % EXPERTS, second)
    first = jnp.where(forced, full_expert, first)
    return jnp.stack([first, second], axis=1).astype(jnp.int32)


def block_levels(own_key, extent, cuts, low, high):
    def one(axis_at, shards_of):
        steps = jax.random.uniform(jax.random.fold_in(jax.random.fold_in(own_key, 6), axis_at), (shards_of,), jnp.float32, low / len(cuts), high / len(cuts))
        return jnp.repeat(jnp.exp(steps), extent[axis_at] // shards_of).reshape((-1,) + (1,) * (len(extent) - axis_at - 1))

    loudness = one(*cuts[0])
    for cut in cuts[1:]:
        loudness = loudness * one(*cut)
    return loudness


def bell_draw(stream_key, shape, deviation, limit, cuts=(), held_as=jnp.bfloat16):
    result = jax.random.normal(stream_key, shape, jnp.float32) * deviation
    if len(cuts) > 0:
        result = block_levels(stream_key, shape, cuts, -0.22, 0.18) * result
    return jnp.clip(result, min=-limit, max=limit).astype(held_as)


def setup_inputs(seed: int = 0) -> dict:
    splits = jax.random.split(jax.random.key(seed), 8)
    return {
        "tokens": bell_draw(splits[0], (TOKENS, D), 1.0, 6.0, ((0, 32),)),
        "cotangent": bell_draw(splits[1], (TOKENS, D), 1.0, 6.0, ((0, 32),)),
        "routes": draw_routes(jax.random.fold_in(splits[7], 71), 0),
        "route_weights": jnp.clip(0.1 + 0.9 * jax.random.uniform(splits[3], (TOKENS, 2), jnp.float32) ** block_levels(splits[3], (TOKENS, 2), ((0, 32),), -0.2, 0.2), 0.1, 1.0),
        "capacity": draw_capacity(jax.random.fold_in(splits[7], 71), 0),
        "w_in": bell_draw(splits[5], (EXPERTS, 2, FF, D), D ** -0.5, 0.125, ((0, 8), (2, 4))),
        "w_down": bell_draw(splits[6], (EXPERTS, FF, D), FF ** -0.5, 0.15625, ((0, 8), (1, 4))),
    }


def expert_math(inputs, scaled, weights_in, weights_down):
    gate_value = jnp.dot(inputs, weights_in[0].T, preferred_element_type=jnp.float32)
    up_value = jnp.dot(inputs, weights_in[1].T, preferred_element_type=jnp.float32)
    sig_gate = jax.nn.sigmoid(gate_value)
    act_gate = gate_value * sig_gate
    hidden = (act_gate * up_value).astype(jnp.bfloat16)
    expert_out = jnp.dot(hidden, weights_down, preferred_element_type=jnp.float32).astype(jnp.bfloat16)
    hidden_grad = jnp.dot(scaled, weights_down.T, preferred_element_type=jnp.float32)
    slope_gate = sig_gate * (1.0 + gate_value * (1.0 - sig_gate))
    gate_grad = (hidden_grad * up_value * slope_gate).astype(jnp.bfloat16)
    up_grad = (hidden_grad * act_gate).astype(jnp.bfloat16)
    gate_weight_grad = jnp.dot(gate_grad.T, inputs, preferred_element_type=jnp.float32)
    up_weight_grad = jnp.dot(up_grad.T, inputs, preferred_element_type=jnp.float32)
    down_weight_grad = jnp.dot(hidden.T, scaled, preferred_element_type=jnp.float32)
    slot_grad = jnp.dot(gate_grad, weights_in[0], preferred_element_type=jnp.float32) + jnp.dot(up_grad, weights_in[1], preferred_element_type=jnp.float32)
    in_grad = jnp.stack([gate_weight_grad, up_weight_grad], axis=0).astype(jnp.bfloat16)
    return expert_out, slot_grad.astype(jnp.bfloat16), in_grad, down_weight_grad.astype(jnp.bfloat16)


def reference(tokens, cotangent, routes, route_weights, capacity, w_in, w_down):
    num_blocks = TOKENS // TOK_DEV
    per_block = 2 * TOK_DEV
    flat_expert = routes.reshape(num_blocks, per_block)
    expert_ids = jnp.arange(EXPERTS, dtype=jnp.int32)
    onehot = (flat_expert[:, :, None] == expert_ids[None, None, :]).astype(jnp.int32)
    earlier = jnp.cumsum(onehot, axis=1) - onehot
    route_rank = jnp.sum(earlier * onehot, axis=2)
    cap_limit = capacity[flat_expert]
    kept_mask = route_rank < cap_limit
    total_slots = num_blocks * CAP
    block_ids = jnp.arange(num_blocks, dtype=jnp.int32)[:, None]
    dummy = EXPERTS * total_slots
    slot_target = jnp.where(kept_mask, flat_expert * total_slots + block_ids * CAP + route_rank, dummy).astype(jnp.int32)
    route_count = 2 * TOKENS
    route_ids = jnp.arange(route_count, dtype=jnp.int32)
    slot_owner = jnp.full((dummy + 1,), route_count, jnp.int32).at[slot_target.reshape(-1)].set(route_ids)[:dummy]
    slot_owner = slot_owner.reshape(EXPERTS, total_slots)
    padded_tokens = jnp.concatenate([tokens, jnp.zeros((1, D), tokens.dtype)], axis=0)
    padded_cot = jnp.concatenate([cotangent, jnp.zeros((1, D), cotangent.dtype)], axis=0)
    padded_weights = jnp.concatenate([route_weights.reshape(-1), jnp.zeros((1,), route_weights.dtype)], axis=0)

    def per_expert(items):
        owner_row, weights_in, weights_down = items
        token_of = (owner_row // 2).astype(jnp.int32)
        inputs = padded_tokens[token_of]
        scaled = (padded_weights[owner_row][:, None] * padded_cot[token_of].astype(jnp.float32)).astype(jnp.bfloat16)
        return expert_math(inputs, scaled, weights_in, weights_down)

    slot_out, slot_grad, d_w_in, d_w_down = lax.map(per_expert, (slot_owner, w_in, w_down))
    flat_out = jnp.concatenate([slot_out.reshape(dummy, D), jnp.zeros((1, D), slot_out.dtype)], axis=0)
    flat_grad = jnp.concatenate([slot_grad.reshape(dummy, D), jnp.zeros((1, D), slot_grad.dtype)], axis=0)
    target_flat = slot_target.reshape(-1)
    out_route = flat_out[target_flat].reshape(TOKENS, 2, D).astype(jnp.float32)
    grad_route = flat_grad[target_flat].reshape(TOKENS, 2, D).astype(jnp.float32)
    mixed = jnp.sum(route_weights[:, :, None] * out_route, axis=1).astype(jnp.bfloat16)
    d_route_weights = jnp.sum(out_route * cotangent.astype(jnp.float32)[:, None, :], axis=2)
    d_tokens = jnp.sum(grad_route, axis=1).astype(jnp.bfloat16)
    return mixed, d_tokens, d_route_weights, d_w_in, d_w_down
```

```python
import functools

import jax
import jax.numpy as jnp
from jax import lax
from jax.experimental import pallas as pl
from jax.experimental.pallas import tpu as pltpu
from jax.sharding import PartitionSpec as P

MESH = pl.DeviceIdType.MESH
OWN, XN, DG, YN = 0, 1, 2, 3


def flip(value, amount, bits):
    out = 0
    for b in range(bits):
        w = 1 << b
        out = out + ((value // w + amount // w) % 2) * w
    return out


def dot_nt(a, b):
    return lax.dot_general(a, b, (((1,), (1,)), ((), ())), preferred_element_type=jnp.float32)


def dot_nn(a, b):
    return lax.dot_general(a, b, (((1,), (0,)), ((), ())), preferred_element_type=jnp.float32)


def dot_tn(a, b):
    return lax.dot_general(a, b, (((0,), (0,)), ((), ())), preferred_element_type=jnp.float32)


def moe_kernel(
    n, tok, cot, pick, rw_slot, comb, comb_hi, comb_lo, w_in, w_down,
    mixed, d_tok, d_slot, d_in, d_down,
    xb, cb, ob, gb, sx, sc, r1o, r1g, r2o, r2g, bo, bg,
    wi, wd, gate, up, hid, gg, ug, dwi, dwd,
    s_a, r_a, s_x, r_x, s_y, r_y, s_d, r_d, s_1, r_1, s_2, r_2, s_b, r_b, s_w,
):
    bits = n.bit_length() - 1
    g = lax.axis_index("dp")
    e = lax.axis_index("expert")
    nx = {"dp": flip(g, 1, 2)}
    ny = {"dp": flip(g, 2, 2)}
    slots = xb.shape[2]
    width = xb.shape[3]
    ff = wd.shape[0]
    rows = n * slots
    half = n // 2
    cw = width // 4
    cols = [pl.ds(i * cw, cw) for i in range(4)]
    bf = jnp.bfloat16
    f32 = jnp.float32

    def peer(d):
        return {"expert": flip(e, d, bits)}

    def rcopy(src, dst, s, r, dev):
        return pltpu.make_async_remote_copy(
            src_ref=src, dst_ref=dst, send_sem=s, recv_sem=r, device_id=dev, device_id_type=MESH
        )

    gather = ((sx, xb), (sc, cb))
    reduce = ((ob, r1o, r2o, bo), (gb, r1g, r2g, bg))

    def send_a(i, d):
        s, b = gather[i]
        return rcopy(s.at[d], b.at[OWN, d], s_a.at[i, d], r_a.at[i, d], peer(d))

    def send_x(i, d):
        b = gather[i][1]
        return rcopy(b.at[OWN, d], b.at[XN, d], s_x.at[i, d], r_x.at[i, d], nx)

    def send_y(i, d):
        b = gather[i][1]
        return rcopy(b.at[OWN, d], b.at[YN, d], s_y.at[i, d], r_y.at[i, d], ny)

    def send_d(i, d, odd):
        b = gather[i][1]
        if odd:
            return rcopy(b.at[YN, d], b.at[DG, d], s_d.at[i, d], r_d.at[i, d], nx)
        return rcopy(b.at[XN, d], b.at[DG, d], s_d.at[i, d], r_d.at[i, d], ny)

    def send_1(i, d, odd):
        b, r1 = reduce[i][:2]
        if odd:
            return rcopy(b.at[pl.ds(DG, 2), d], r1.at[d], s_1.at[i, d], r_1.at[i, d], ny)
        return rcopy(b.at[pl.ds(XN, 2), d], r1.at[d], s_1.at[i, d], r_1.at[i, d], nx)

    def send_2(i, d, odd):
        b, _, r2, _ = reduce[i]
        if odd:
            return rcopy(b.at[XN, d], r2.at[d], s_2.at[i, d], r_2.at[i, d], nx)
        return rcopy(b.at[YN, d], r2.at[d], s_2.at[i, d], r_2.at[i, d], ny)

    def send_b(i, d):
        b, _, _, back = reduce[i]
        return rcopy(b.at[OWN, d], back.at[d], s_b.at[i, d], r_b.at[i, d], peer(d))

    def forward(i, d, odd):
        (send_y if odd else send_x)(i, d).wait_recv()
        send_d(i, d, odd).start()

    def middle(i, d, odd):
        b, r1 = reduce[i][:2]
        send_1(i, d, odd).wait_recv()
        at, got = (XN, 0) if odd else (YN, 1)
        b[at, d] = (b[at, d].astype(f32) + r1[d, got].astype(f32)).astype(bf)
        send_2(i, d, odd).start()

    def finish(i, d, odd):
        b, r1, r2, back = reduce[i]
        send_2(i, d, odd).wait_recv()
        got = 1 if odd else 0
        total = b[OWN, d].astype(f32) + r1[d, got].astype(f32) + r2[d].astype(f32)
        b[OWN, d] = total.astype(bf)

    def load_w():
        return (
            pltpu.make_async_copy(w_in, wi, s_w.at[0]),
            pltpu.make_async_copy(w_down, wd, s_w.at[1]),
        )

    def group_wait(i, pos):
        if pos == XN:
            for d in range(1, n, 2):
                send_x(i, d).wait_recv()
        if pos == YN:
            for d in range(0, n, 2):
                send_y(i, d).wait_recv()
        if pos == DG:
            for d in range(n):
                send_d(i, d, d % 2).wait_recv()

    barrier = pltpu.get_barrier_semaphore()
    for d in range(1, n):
        pl.semaphore_signal(barrier, inc=1, device_id=peer(d), device_id_type=MESH)
    for dev in (nx, ny):
        pl.semaphore_signal(barrier, inc=1, device_id=dev, device_id_type=MESH)
    for c in load_w():
        c.start()

    def bucket(i, d):
        at = pl.ds(d * slots, slots)
        source = (tok, cot)[i]
        for c in cols:
            v = dot_nn(pick[at, :], source[:, c])
            if i:
                v = v * rw_slot[at, :]
            gather[i][0][d, :, c] = v.astype(bf)

    bucket(0, 0)
    xb[OWN, 0] = sx[0]
    pl.semaphore_wait(barrier, n + 1)
    send_x(0, 0).start()
    send_y(0, 0).start()

    @pl.loop(1, n)
    def _(d):
        bucket(0, d)
        send_a(0, d).start()

    @pl.loop(0, n)
    def _(d):
        bucket(1, d)

    cb[OWN, 0] = sc[0]

    lag = 2
    for k in range(n + lag):
        if k < n:
            if k:
                send_a(0, k).wait_recv()
                send_x(0, k).start()
                send_y(0, k).start()
                send_a(1, k).start()
        if k >= lag:
            forward(0, k - lag, (k - lag) % 2)

    for c in load_w():
        c.wait()

    per = half // 4

    def expert_fwd(q):
        at = pl.ds(q * rows, rows)
        x = xb[q].reshape(rows, width)
        gv = dot_nt(x, wi[0])
        uv = dot_nt(x, wi[1])
        gate[at, :] = gv
        up[at, :] = uv
        h = (gv * jax.nn.sigmoid(gv) * uv).astype(bf)
        hid[at, :] = h
        for c in cols:
            ob[q, :, :, c] = dot_nn(h, wd[:, c]).astype(bf).reshape(n, slots, cw)

    def expert_bwd(q):
        at = pl.ds(q * rows, rows)
        hg = dot_nt(cb[q].reshape(rows, width), wd[...])
        gv = gate[at, :]
        uv = up[at, :]
        sg = jax.nn.sigmoid(gv)
        a = (hg * uv * (sg * (1.0 + gv * (1.0 - sg)))).astype(bf)
        b = (hg * (gv * sg)).astype(bf)
        gg[at, :] = a
        ug[at, :] = b
        for c in cols:
            v = dot_nn(a, wi[0, :, c]) + dot_nn(b, wi[1, :, c])
            gb[q, :, :, c] = v.astype(bf).reshape(n, slots, cw)

    send_x(1, 0).start()
    send_y(1, 0).start()

    @pl.loop(0, 4)
    def _(q):
        for p in range(per):
            for odd in (0, 1):
                d = (q * per + p) * 2 + odd

                @pl.when(d > 0)
                def _():
                    send_a(1, d).wait_recv()
                    send_x(1, d).start()
                    send_y(1, d).start()

        @pl.when(q > 0)
        def _():
            for p in range(per):
                for odd in (0, 1):
                    forward(1, ((q - 1) * per + p) * 2 + odd, odd)

        for pos in (XN, DG, YN):

            @pl.when(q == pos)
            def _():
                group_wait(0, pos)

        expert_fwd(q)

    for d in range(n):
        if d >= n - 2 * per:
            forward(1, d, d % 2)
        send_1(0, d, d % 2).start()

    @pl.loop(0, 4)
    def _(q):
        for pos in (XN, DG, YN):

            @pl.when(q == pos - 1)
            def _():
                group_wait(1, pos)

        expert_bwd((q + 1) % 4)

        @pl.when(q == 2)
        def _():
            for d in range(n):
                send_1(1, d, d % 2).start()

        for p in range(per):
            for odd in (0, 1):
                middle(0, (q * per + p) * 2 + odd, odd)

    @pl.loop(0, 4)
    def _(q):
        c = pl.ds(pl.multiple_of(q * cw, cw), cw)
        for p in range(per):
            for odd in (0, 1):
                d = (q * per + p) * 2 + odd
                finish(0, d, odd)

                @pl.when(d > 0)
                def _():
                    send_b(0, d).start()

                middle(1, d, odd)
        x = xb[:, :, :, c].reshape(4 * rows, cw)
        dwi[0, :, c] = dot_tn(gg[...], x).astype(bf)
        dwi[1, :, c] = dot_tn(ug[...], x).astype(bf)
        dwd[:, c] = dot_tn(hid[...], cb[:, :, :, c].reshape(4 * rows, cw)).astype(bf)

    def store_w():
        return (
            pltpu.make_async_copy(dwi, d_in, s_w.at[2]),
            pltpu.make_async_copy(dwd, d_down, s_w.at[3]),
        )

    for c in store_w():
        c.start()

    @pl.loop(0, half)
    def _(h):
        for odd in (0, 1):
            d = h * 2 + odd
            finish(1, d, odd)

            @pl.when(d > 0)
            def _():
                send_b(1, d).start()

    bo[0] = ob[OWN, 0]
    bg[0] = gb[OWN, 0]
    for d in range(1, n):
        send_b(0, d).wait_recv()
    back = bo[...].reshape(rows, width)
    acc = jnp.zeros((rows, 1), f32)
    for c in cols:
        part = back[:, c.start : c.start + cw]
        mixed[:, c] = (dot_nn(comb_hi[...], part) + dot_nn(comb_lo[...], part)).astype(bf)
        acc = acc + jnp.sum(part.astype(f32) * dot_nn(pick[...], cot[:, c]), axis=1, keepdims=True)
    d_slot[...] = acc
    for d in range(1, n):
        send_b(1, d).wait_recv()
    for c in cols:
        d_tok[:, c] = dot_nn(comb[...], bg[:, :, c].reshape(rows, cw)).astype(bf)

    for i in (0, 1):
        for d in range(n):
            if d:
                send_a(i, d).wait_send()
                send_b(i, d).wait_send()
            send_x(i, d).wait_send()
            send_y(i, d).wait_send()
            send_d(i, d, d % 2).wait_send()
            send_1(i, d, d % 2).wait_send()
            send_2(i, d, d % 2).wait_send()
    for c in store_w():
        c.wait()


def fused(tokens, cotangent, routes, route_weights, capacity, w_in, w_down):
    n = capacity.shape[0]
    tok_rows, width = tokens.shape
    slots = tok_rows * 2 // n
    ff = w_down.shape[1]
    rows = n * slots
    bf, f32, i32 = jnp.bfloat16, jnp.float32, jnp.int32
    e = lax.axis_index("expert")
    flat = routes.reshape(-1)
    count = 2 * tok_rows
    same = flat[:, None] == flat[None, :]
    before = lax.broadcasted_iota(i32, (count, count), 1) < lax.broadcasted_iota(i32, (count, count), 0)
    rank = jnp.sum((same & before).astype(i32), axis=1).reshape(tok_rows, 2)
    row = lax.iota(i32, rows)
    row_expert = e ^ (row // slots)
    row_rank = row % slots
    row_cap = jnp.sum(
        jnp.where(row_expert[:, None] == lax.iota(i32, n)[None, :], capacity[None, :], 0), axis=1
    )
    row_ok = row_rank < row_cap
    hit = (
        (routes[:, :, None] == row_expert)
        & (rank[:, :, None] == row_rank)
        & row_ok
    )
    comb = (hit[:, 0] | hit[:, 1]).astype(bf)
    pick = comb.T
    weighted = jnp.sum(jnp.where(hit, route_weights[:, :, None], 0.0), axis=1)
    comb_hi = weighted.astype(bf)
    comb_lo = (weighted - comb_hi.astype(f32)).astype(bf)
    rw_slot = jnp.sum(weighted, axis=0)[:, None]
    vm = pl.BlockSpec(memory_space=pltpu.VMEM)
    hbm = pl.BlockSpec(memory_space=pl.ANY)
    big = pltpu.VMEM((4, n, slots, width), bf)
    piece = pltpu.VMEM((n, slots, width), bf)
    two = pltpu.VMEM((n, 2, slots, width), bf)
    sem = pltpu.SemaphoreType.DMA((2, n))
    mixed, d_tok, d_slot, d_in, d_down = pl.pallas_call(
        functools.partial(moe_kernel, n),
        out_shape=(
            jax.ShapeDtypeStruct((tok_rows, width), bf),
            jax.ShapeDtypeStruct((tok_rows, width), bf),
            jax.ShapeDtypeStruct((rows, 1), f32),
            jax.ShapeDtypeStruct((2, ff, width), bf),
            jax.ShapeDtypeStruct((ff, width), bf),
        ),
        in_specs=[vm] * 7 + [hbm] * 2,
        out_specs=(vm, vm, vm, hbm, hbm),
        scratch_shapes=[
            big, big, big, big, piece, piece, two, two, piece, piece, piece, piece,
            pltpu.VMEM((2, ff, width), bf),
            pltpu.VMEM((ff, width), bf),
            pltpu.VMEM((4 * rows, ff), f32),
            pltpu.VMEM((4 * rows, ff), f32),
            pltpu.VMEM((4 * rows, ff), bf),
            pltpu.VMEM((4 * rows, ff), bf),
            pltpu.VMEM((4 * rows, ff), bf),
            pltpu.VMEM((2, ff, width), bf),
            pltpu.VMEM((ff, width), bf),
        ]
        + [sem] * 14
        + [pltpu.SemaphoreType.DMA((4,))],
        compiler_params=pltpu.CompilerParams(
            collective_id=0, has_side_effects=True, vmem_limit_bytes=60 * 2**20
        ),
    )(tokens, cotangent, pick, rw_slot, comb, comb_hi, comb_lo, w_in[0], w_down[0])
    d_rw = jnp.sum(jnp.where(hit, d_slot[:, 0], 0.0), axis=2)
    return mixed, d_tok, d_rw, d_in[None], d_down[None]


def expert_forward(inputs, weights_in, weights_down):
    gate_value = jnp.einsum(
        "gecd,ehd->gech", inputs, weights_in[:, 0], preferred_element_type=jnp.float32
    )
    up_value = jnp.einsum(
        "gecd,ehd->gech", inputs, weights_in[:, 1], preferred_element_type=jnp.float32
    )
    sig_gate = jax.nn.sigmoid(gate_value)
    act_gate = gate_value * sig_gate
    hidden = (act_gate * up_value).astype(jnp.bfloat16)
    partial_out = jnp.einsum(
        "gech,ehd->gecd", hidden, weights_down, preferred_element_type=jnp.float32
    )
    return ((gate_value, up_value, sig_gate, act_gate, hidden), partial_out)


def expert_backward(inputs, scaled, weights_in, weights_down, saved):
    gate_value, up_value, sig_gate, act_gate, hidden = saved
    hidden_grad = jnp.einsum(
        "gecd,ehd->gech", scaled, weights_down, preferred_element_type=jnp.float32
    )
    slope_gate = sig_gate * (1.0 + gate_value * (1.0 - sig_gate))
    gate_grad = (hidden_grad * up_value * slope_gate).astype(jnp.bfloat16)
    up_grad = (hidden_grad * act_gate).astype(jnp.bfloat16)
    gate_weight_grad = jnp.einsum(
        "gech,gecd->ehd", gate_grad, inputs, preferred_element_type=jnp.float32
    )
    up_weight_grad = jnp.einsum(
        "gech,gecd->ehd", up_grad, inputs, preferred_element_type=jnp.float32
    )
    down_weight_grad = jnp.einsum(
        "gech,gecd->ehd", hidden, scaled, preferred_element_type=jnp.float32
    )
    input_grad = jnp.einsum(
        "gech,ehd->gecd", gate_grad, weights_in[:, 0], preferred_element_type=jnp.float32
    )
    input_grad = input_grad + jnp.einsum(
        "gech,ehd->gecd", up_grad, weights_in[:, 1], preferred_element_type=jnp.float32
    )
    return (jnp.stack([gate_weight_grad, up_weight_grad], axis=1), down_weight_grad, input_grad)


def body(tokens, cotangent, routes, route_weights, capacity, w_in, w_down):
    experts = capacity.shape[0]
    expert_devs = lax.axis_size("expert")
    local_experts = experts // expert_devs
    tok_rows = tokens.shape[0]
    width = tokens.shape[1]
    slots = tok_rows * 2 // experts
    power = experts & (experts - 1) == 0 and experts % 8 == 0
    if local_experts == 1 and slots % 16 == 0 and power and lax.axis_size("dp") == 4:
        return fused(tokens, cotangent, routes, route_weights, capacity, w_in, w_down)
    flat_expert = routes.reshape(-1)
    expert_ids = jnp.arange(experts, dtype=jnp.int32)
    onehot = (flat_expert[:, None] == expert_ids[None, :]).astype(jnp.int32)
    ids = jnp.arange(flat_expert.shape[0], dtype=jnp.int32)
    before = (ids[None, :] < ids[:, None]).astype(jnp.float32)
    earlier = jnp.dot(before, onehot.astype(jnp.float32)).astype(jnp.int32)
    route_rank = jnp.sum(earlier * onehot, axis=1)
    cap_limit = jnp.sum(onehot * capacity[None, :], axis=1)
    kept_mask = route_rank < cap_limit
    dummy = experts * slots
    slot_target = jnp.where(kept_mask, flat_expert * slots + route_rank, dummy)
    route_count = 2 * tok_rows
    route_ids = jnp.arange(route_count, dtype=jnp.int32)
    slot_owner = (
        jnp.full((dummy + 1,), route_count, jnp.int32).at[slot_target].set(route_ids)[:dummy]
    )
    token_of = slot_owner // 2
    padded_tokens = jnp.concatenate([tokens, jnp.zeros((1, width), tokens.dtype)], axis=0)
    padded_cot = jnp.concatenate([cotangent, jnp.zeros((1, width), cotangent.dtype)], axis=0)
    padded_weights = jnp.concatenate(
        [route_weights.reshape(-1), jnp.zeros((1,), jnp.float32)], axis=0
    )
    bucket_shape = (expert_devs, local_experts, slots, width)
    send_inputs = padded_tokens[token_of].reshape(bucket_shape)
    send_scaled = (
        (padded_weights[slot_owner][:, None] * padded_cot[token_of].astype(jnp.float32))
        .astype(jnp.bfloat16)
        .reshape(bucket_shape)
    )
    recv_inputs = lax.all_to_all(send_inputs, "expert", split_axis=0, concat_axis=0, tiled=True)
    use_inputs = lax.all_gather(recv_inputs, "dp", axis=0, tiled=True)
    saved, partial_out = expert_forward(use_inputs, w_in, w_down)
    out_local = lax.psum_scatter(
        partial_out.astype(jnp.bfloat16), "dp", scatter_dimension=0, tiled=True
    )
    out_back = lax.all_to_all(out_local, "expert", split_axis=0, concat_axis=0, tiled=True)
    recv_scaled = lax.all_to_all(send_scaled, "expert", split_axis=0, concat_axis=0, tiled=True)
    use_scaled = lax.all_gather(recv_scaled, "dp", axis=0, tiled=True)
    in_weight_grad, down_weight_grad, input_grad = expert_backward(
        use_inputs, use_scaled, w_in, w_down, saved
    )
    grad_local = lax.psum_scatter(
        input_grad.astype(jnp.bfloat16), "dp", scatter_dimension=0, tiled=True
    )
    grad_back = lax.all_to_all(grad_local, "expert", split_axis=0, concat_axis=0, tiled=True)
    flat_out = jnp.concatenate(
        [out_back.reshape(dummy, width), jnp.zeros((1, width), jnp.bfloat16)], axis=0
    )
    flat_grad = jnp.concatenate(
        [grad_back.reshape(dummy, width), jnp.zeros((1, width), jnp.bfloat16)], axis=0
    )
    out_route = flat_out[slot_target].reshape(tok_rows, 2, width).astype(jnp.float32)
    grad_route = flat_grad[slot_target].reshape(tok_rows, 2, width).astype(jnp.float32)
    mixed = jnp.sum(route_weights[:, :, None] * out_route, axis=1).astype(jnp.bfloat16)
    d_route_weights = jnp.sum(out_route * cotangent.astype(jnp.float32)[:, None, :], axis=2)
    d_tokens = jnp.sum(grad_route, axis=1).astype(jnp.bfloat16)
    return (
        mixed,
        d_tokens,
        d_route_weights,
        in_weight_grad.astype(jnp.bfloat16),
        down_weight_grad.astype(jnp.bfloat16),
    )


def solution(mesh):
    placed = (
        P(("dp", "expert"), None),
        P(("dp", "expert"), None),
        P(("dp", "expert"), None),
        P(("dp", "expert"), None),
        P(),
        P("expert", None, "dp", None),
        P("expert", "dp", None),
    )
    return jax.shard_map(
        body,
        mesh=mesh,
        in_specs=placed,
        out_specs=(
            P(("dp", "expert"), None),
            P(("dp", "expert"), None),
            P(("dp", "expert"), None),
            P("expert", None, "dp", None),
            P("expert", "dp", None),
        ),
        check_vma=False,
    )
```

```python
import functools

import jax
import jax.numpy as jnp
from jax import lax
from jax.experimental import pallas as pl
from jax.experimental.pallas import tpu as pltpu
from jax.sharding import PartitionSpec as P

MESH = pl.DeviceIdType.MESH
OWN, XN, DG, YN = 0, 1, 2, 3


def flip(value, amount, bits):
    out = 0
    for b in range(bits):
        w = 1 << b
        out = out + ((value // w + amount // w) % 2) * w
    return out


def offset(d):
    q = d // 2
    low, high = q % 2, (q // 2) % 2
    even = d - (q % 4) * 2 + 2 * (2 * ((low + high) % 2) + high)
    odd = d % 2
    return even * (1 - odd) + d * odd


def dot_nt(a, b):
    return lax.dot_general(a, b, (((1,), (1,)), ((), ())), preferred_element_type=jnp.float32)


def dot_nn(a, b):
    return lax.dot_general(a, b, (((1,), (0,)), ((), ())), preferred_element_type=jnp.float32)


def dot_tn(a, b):
    return lax.dot_general(a, b, (((0,), (0,)), ((), ())), preferred_element_type=jnp.float32)


def moe_kernel(
    n, tok, cot, route, rw, cap, w_in, w_down,
    mixed, d_tok, d_rw, d_in, d_down,
    pick, first, comb_hi, comb_lo, rw_slot,
    xb, cb, ob, gb, sx, sc, r1o, r1g, r2o, r2g, bo, bg,
    wi, wd, gate, up, hid, gg, ug, dwi, dwd,
    s_a, r_a, s_x, r_x, s_y, r_y, s_d, r_d, s_1, r_1, s_2, r_2, s_b, r_b, s_w,
):
    bits = n.bit_length() - 1
    g = lax.axis_index("dp")
    e = lax.axis_index("expert")
    nx = {"dp": flip(g, 1, 2)}
    ny = {"dp": flip(g, 2, 2)}
    slots = xb.shape[2]
    width = xb.shape[3]
    ff = wd.shape[0]
    rows = n * slots
    half = n // 2
    cw = width // 4
    cols = [pl.ds(i * cw, cw) for i in range(4)]
    bf = jnp.bfloat16
    f32 = jnp.float32

    def peer(d):
        return {"expert": flip(e, offset(d), bits)}

    def rcopy(src, dst, s, r, dev):
        return pltpu.make_async_remote_copy(
            src_ref=src, dst_ref=dst, send_sem=s, recv_sem=r, device_id=dev, device_id_type=MESH
        )

    gather = ((sx, xb), (sc, cb))
    reduce = ((ob, r1o, r2o, bo), (gb, r1g, r2g, bg))

    def send_a(i, d):
        s, b = gather[i]
        return rcopy(s.at[d], b.at[OWN, d], s_a.at[i, d], r_a.at[i, d], peer(d))

    def send_x(i, d):
        b = gather[i][1]
        return rcopy(b.at[OWN, d], b.at[XN, d], s_x.at[i, d], r_x.at[i, d], nx)

    def send_y(i, d):
        b = gather[i][1]
        return rcopy(b.at[OWN, d], b.at[YN, d], s_y.at[i, d], r_y.at[i, d], ny)

    def send_d(i, d, odd):
        b = gather[i][1]
        if odd:
            return rcopy(b.at[YN, d], b.at[DG, d], s_d.at[i, d], r_d.at[i, d], nx)
        return rcopy(b.at[XN, d], b.at[DG, d], s_d.at[i, d], r_d.at[i, d], ny)

    def send_1(i, d, odd):
        b, r1 = reduce[i][:2]
        if odd:
            return rcopy(b.at[pl.ds(DG, 2), d], r1.at[d], s_1.at[i, d], r_1.at[i, d], ny)
        return rcopy(b.at[pl.ds(XN, 2), d], r1.at[d], s_1.at[i, d], r_1.at[i, d], nx)

    def send_2(i, d, odd):
        b, _, r2, _ = reduce[i]
        if odd:
            return rcopy(b.at[XN, d], r2.at[d], s_2.at[i, d], r_2.at[i, d], nx)
        return rcopy(b.at[YN, d], r2.at[d], s_2.at[i, d], r_2.at[i, d], ny)

    def send_b(i, d):
        b, _, _, back = reduce[i]
        return rcopy(b.at[OWN, d], back.at[d], s_b.at[i, d], r_b.at[i, d], peer(d))

    def forward(i, d, odd):
        (send_y if odd else send_x)(i, d).wait_recv()
        send_d(i, d, odd).start()

    def middle(i, d, odd):
        b, r1 = reduce[i][:2]
        send_1(i, d, odd).wait_recv()
        at, got = (XN, 0) if odd else (YN, 1)
        b[at, d] = (b[at, d].astype(f32) + r1[d, got].astype(f32)).astype(bf)
        send_2(i, d, odd).start()

    def finish(i, d, odd):
        b, r1, r2, back = reduce[i]
        send_2(i, d, odd).wait_recv()
        got = 1 if odd else 0
        total = b[OWN, d].astype(f32) + r1[d, got].astype(f32) + r2[d].astype(f32)
        b[OWN, d] = total.astype(bf)

    def load_w():
        return (
            pltpu.make_async_copy(w_in, wi, s_w.at[0]),
            pltpu.make_async_copy(w_down, wd, s_w.at[1]),
        )

    def group_wait(i, pos):
        if pos == XN:
            for d in range(1, n, 2):
                send_x(i, d).wait_recv()
        if pos == YN:
            for d in range(0, n, 2):
                send_y(i, d).wait_recv()
        if pos == DG:
            for d in range(n):
                send_d(i, d, d % 2).wait_recv()

    barrier = pltpu.get_barrier_semaphore()
    for d in range(1, n):
        pl.semaphore_signal(barrier, inc=1, device_id=peer(d), device_id_type=MESH)
    for dev in (nx, ny):
        pl.semaphore_signal(barrier, inc=1, device_id=dev, device_id_type=MESH)
    for c in load_w():
        c.start()

    def bucket(i, d):
        at = pl.ds(d * slots, slots)
        source = (tok, cot)[i]
        for c in cols:
            v = dot_nn(pick[at, :], source[:, c])
            if i:
                v = v * rw_slot[at, :]
            gather[i][0][d, :, c] = v.astype(bf)

    toks = tok.shape[0]
    expert = jnp.bitwise_xor(offset(lax.broadcasted_iota(jnp.int32, (n, toks), 0)), e)
    m0 = route[0:1, :] == expert
    m1 = route[1:2, :] == expert
    limit = jnp.zeros((n, toks), jnp.int32)
    for x in range(n):
        limit = jnp.where(expert == x, cap[x], limit)
    upper = jnp.where(
        lax.broadcasted_iota(jnp.int32, (toks, toks), 0)
        < lax.broadcasted_iota(jnp.int32, (toks, toks), 1),
        1.0,
        0.0,
    ).astype(bf)
    rank = dot_nn(jnp.where(m0 | m1, 1.0, 0.0).astype(bf), upper)
    rank = jnp.where(rank < limit.astype(f32), rank, -1.0)
    v0 = jnp.where(m0, rank, -1.0)
    v1 = jnp.where(m1, rank, -1.0)
    slot = lax.broadcasted_iota(jnp.int32, (slots, toks), 0).astype(f32)
    for d in range(n):
        at = pl.ds(d * slots, slots)
        p0 = v0[d : d + 1, :] == slot
        p1 = v1[d : d + 1, :] == slot
        wt = jnp.where(p0, rw[0:1, :], 0.0) + jnp.where(p1, rw[1:2, :], 0.0)
        hi = wt.astype(bf)
        pick[at, :] = jnp.where(p0 | p1, 1.0, 0.0).astype(bf)
        first[at, :] = jnp.where(p0, 1.0, 0.0)
        comb_hi[at, :] = hi
        comb_lo[at, :] = (wt - hi.astype(f32)).astype(bf)
        rw_slot[at, :] = jnp.sum(wt, axis=1, keepdims=True)

    def expert_fwd(q):
        at = pl.ds(q * rows, rows)
        x = xb[q].reshape(rows, width)
        gv = dot_nt(x, wi[0])
        uv = dot_nt(x, wi[1])
        gate[at, :] = gv
        up[at, :] = uv
        h = (gv * jax.nn.sigmoid(gv) * uv).astype(bf)
        hid[at, :] = h
        for c in cols:
            ob[q, :, :, c] = dot_nn(h, wd[:, c]).astype(bf).reshape(n, slots, cw)

    def expert_bwd(q):
        at = pl.ds(q * rows, rows)
        hg = dot_nt(cb[q].reshape(rows, width), wd[...])
        gv = gate[at, :]
        uv = up[at, :]
        sg = jax.nn.sigmoid(gv)
        a = (hg * uv * (sg * (1.0 + gv * (1.0 - sg)))).astype(bf)
        b = (hg * (gv * sg)).astype(bf)
        gg[at, :] = a
        ug[at, :] = b
        for c in cols:
            v = dot_nn(a, wi[0, :, c]) + dot_nn(b, wi[1, :, c])
            gb[q, :, :, c] = v.astype(bf).reshape(n, slots, cw)

    def store_w():
        return (
            pltpu.make_async_copy(dwi, d_in, s_w.at[2]),
            pltpu.make_async_copy(dwd, d_down, s_w.at[3]),
        )

    def combine_out():
        bo[0] = ob[OWN, 0]
        for d in range(1, n):
            send_b(0, d).wait_recv()
        back = bo[...].reshape(rows, width)
        acc = jnp.zeros((rows, 1), f32)
        for c in cols:
            part = back[:, c.start : c.start + cw]
            mixed[:, c] = (dot_tn(comb_hi[...], part) + dot_tn(comb_lo[...], part)).astype(bf)
            acc = acc + jnp.sum(part.astype(f32) * dot_nn(pick[...], cot[:, c]), axis=1, keepdims=True)
        one = jnp.sum(acc * first[...], axis=0, keepdims=True)
        d_rw[0:1, :] = one
        d_rw[1:2, :] = jnp.sum(acc * (pick[...].astype(f32) - first[...]), axis=0, keepdims=True)
    def combine_grad():
        bg[0] = gb[OWN, 0]
        for d in range(1, n):
            send_b(1, d).wait_recv()
        for c in cols:
            d_tok[:, c] = dot_tn(pick[...], bg[:, :, c].reshape(rows, cw)).astype(bf)


    def weight_grad(q):
        c = cols[q]
        x = xb[:, :, :, c].reshape(4 * rows, cw)
        dwi[0, :, c] = dot_tn(gg[...], x).astype(bf)
        dwi[1, :, c] = dot_tn(ug[...], x).astype(bf)
        dwd[:, c] = dot_tn(hid[...], cb[:, :, :, c].reshape(4 * rows, cw)).astype(bf)

    def scatter(i, d):
        send_x(i, d).start()
        send_y(i, d).start()

    z_window, lag, r_window, r_lag = 4, 3, 2, 2
    far = [(i, d) for i in (0, 1) for d in range(2, n)]
    order = [(0, 1), (1, 1)] + far
    spread = [(0, 0), (1, 0)] + order

    bucket(0, 0)
    xb[OWN, 0] = sx[0]
    pl.semaphore_wait(barrier, n + 1)
    scatter(0, 0)
    for k, (i, d) in enumerate(order[:z_window]):
        bucket(i, d)
        send_a(i, d).start()
        if k == 0:
            bucket(1, 0)
            cb[OWN, 0] = sc[0]
            scatter(1, 0)
    for c in load_w():
        c.wait()

    last = order.index((0, n - 1))
    fwd_at = {last + 1: OWN, last + 3: XN, last + 4: YN, len(order) - 1: DG}
    steps = len(order)
    done = 0
    for k in range(steps):
        i, d = order[k]
        send_a(i, d).wait_recv()
        scatter(i, d)
        if k + z_window < steps:
            i, d = order[k + z_window]
            bucket(i, d)
            send_a(i, d).start()
        if k + 2 - lag >= 0:
            i, d = spread[k + 2 - lag]
            forward(i, d, d % 2)
            done = k + 3 - lag
        if k in fwd_at:
            group_wait(0, fwd_at[k])
            expert_fwd(fwd_at[k])

    chain = [(i, d) for i in (0, 1) for d in range(n - 1, -1, -1)]
    for i, d in chain[:r_window]:
        send_1(i, d, d % 2).start()
    for i, d in spread[done:]:
        forward(i, d, d % 2)

    def close(i, d):
        finish(i, d, d % 2)
        if d:
            send_b(i, d).start()

    bwd_at = [XN, YN, DG, OWN]
    for k in range(len(chain) + r_lag):
        if k < 4:
            group_wait(1, bwd_at[k])
            expert_bwd(bwd_at[k])
        if k < len(chain):
            i, d = chain[k]
            middle(i, d, d % 2)
            if k + r_window < len(chain):
                i, d = chain[k + r_window]
                send_1(i, d, d % 2).start()
        if k >= r_lag:
            close(*chain[k - r_lag])
        if 5 <= k < 9:
            weight_grad(k - 5)
        if k == 9:
            for c in store_w():
                c.start()
        if k == len(chain) - 2:
            combine_out()
    combine_grad()

    for i in (0, 1):
        for d in range(n):
            if d:
                send_a(i, d).wait_send()
                send_b(i, d).wait_send()
            send_x(i, d).wait_send()
            send_y(i, d).wait_send()
            send_d(i, d, d % 2).wait_send()
            send_1(i, d, d % 2).wait_send()
            send_2(i, d, d % 2).wait_send()
    for c in store_w():
        c.wait()


def land(*arrays):
    cuts = []
    for k, a in enumerate(arrays):
        size = a.shape[-2]
        parts = 2 if size % 32 == 0 else 1
        for lead in range(a.shape[0] if a.ndim == 3 else 1):
            for p in range(parts):
                at = pl.ds(p * (size // parts), size // parts)
                cuts.append((k, (lead, at) if a.ndim == 3 else (at,)))
    m = len(arrays)

    def run(*refs):
        came, went = refs[-2:]
        loads = [
            pltpu.make_async_copy(refs[k].at[at], refs[2 * m + k].at[at], came.at[i])
            for i, (k, at) in enumerate(cuts)
        ]
        stores = [
            pltpu.make_async_copy(refs[2 * m + k].at[at], refs[m + k].at[at], went.at[i])
            for i, (k, at) in enumerate(cuts)
        ]
        for c in loads:
            c.start()
        for a, b in zip(loads, stores):
            a.wait()
            b.start()
        for c in stores:
            c.wait()

    return pl.pallas_call(
        run,
        out_shape=tuple(jax.ShapeDtypeStruct(a.shape, a.dtype) for a in arrays),
        in_specs=[pl.BlockSpec(memory_space=pl.ANY)] * m,
        out_specs=tuple([pl.BlockSpec(memory_space=pl.ANY)] * m),
        scratch_shapes=[pltpu.VMEM(a.shape, a.dtype) for a in arrays]
        + [pltpu.SemaphoreType.DMA((len(cuts),))] * 2,
        compiler_params=pltpu.CompilerParams(vmem_limit_bytes=60 * 2**20),
    )(*arrays)


def fused(tokens, cotangent, routes, route_weights, capacity, w_in, w_down):
    n = capacity.shape[0]
    tok_rows, width = tokens.shape
    slots = tok_rows * 2 // n
    ff = w_down.shape[1]
    rows = n * slots
    bf, f32 = jnp.bfloat16, jnp.float32
    vm = pl.BlockSpec(memory_space=pltpu.VMEM)
    hbm = pl.BlockSpec(memory_space=pl.ANY)
    big = pltpu.VMEM((4, n, slots, width), bf)
    piece = pltpu.VMEM((n, slots, width), bf)
    two = pltpu.VMEM((n, 2, slots, width), bf)
    sem = pltpu.SemaphoreType.DMA((2, n))
    mixed, d_tok, d_rw, d_in, d_down = pl.pallas_call(
        functools.partial(moe_kernel, n),
        out_shape=(
            jax.ShapeDtypeStruct((tok_rows, width), bf),
            jax.ShapeDtypeStruct((tok_rows, width), bf),
            jax.ShapeDtypeStruct((2, tok_rows), f32),
            jax.ShapeDtypeStruct((2, ff, width), bf),
            jax.ShapeDtypeStruct((ff, width), bf),
        ),
        in_specs=[vm] * 4 + [pl.BlockSpec(memory_space=pltpu.SMEM)] + [hbm] * 2,
        out_specs=(vm, vm, vm, hbm, hbm),
        scratch_shapes=[
            pltpu.VMEM((rows, tok_rows), bf),
            pltpu.VMEM((rows, tok_rows), f32),
            pltpu.VMEM((rows, tok_rows), bf),
            pltpu.VMEM((rows, tok_rows), bf),
            pltpu.VMEM((rows, 1), f32),
            big, big, big, big, piece, piece, two, two, piece, piece, piece, piece,
            pltpu.VMEM((2, ff, width), bf),
            pltpu.VMEM((ff, width), bf),
            pltpu.VMEM((4 * rows, ff), f32),
            pltpu.VMEM((4 * rows, ff), f32),
            pltpu.VMEM((4 * rows, ff), bf),
            pltpu.VMEM((4 * rows, ff), bf),
            pltpu.VMEM((4 * rows, ff), bf),
            pltpu.VMEM((2, ff, width), bf),
            pltpu.VMEM((ff, width), bf),
        ]
        + [sem] * 14
        + [pltpu.SemaphoreType.DMA((4,))],
        compiler_params=pltpu.CompilerParams(
            collective_id=0, has_side_effects=True, vmem_limit_bytes=60 * 2**20
        ),
    )(tokens, cotangent, routes.T, route_weights.T, capacity, w_in[0], w_down[0])
    mixed, d_tok, d_in, d_down = land(mixed, d_tok, d_in, d_down)
    return mixed, d_tok, d_rw.T, d_in[None], d_down[None]


def expert_forward(inputs, weights_in, weights_down):
    gate_value = jnp.einsum(
        "gecd,ehd->gech", inputs, weights_in[:, 0], preferred_element_type=jnp.float32
    )
    up_value = jnp.einsum(
        "gecd,ehd->gech", inputs, weights_in[:, 1], preferred_element_type=jnp.float32
    )
    sig_gate = jax.nn.sigmoid(gate_value)
    act_gate = gate_value * sig_gate
    hidden = (act_gate * up_value).astype(jnp.bfloat16)
    partial_out = jnp.einsum(
        "gech,ehd->gecd", hidden, weights_down, preferred_element_type=jnp.float32
    )
    return ((gate_value, up_value, sig_gate, act_gate, hidden), partial_out)


def expert_backward(inputs, scaled, weights_in, weights_down, saved):
    gate_value, up_value, sig_gate, act_gate, hidden = saved
    hidden_grad = jnp.einsum(
        "gecd,ehd->gech", scaled, weights_down, preferred_element_type=jnp.float32
    )
    slope_gate = sig_gate * (1.0 + gate_value * (1.0 - sig_gate))
    gate_grad = (hidden_grad * up_value * slope_gate).astype(jnp.bfloat16)
    up_grad = (hidden_grad * act_gate).astype(jnp.bfloat16)
    gate_weight_grad = jnp.einsum(
        "gech,gecd->ehd", gate_grad, inputs, preferred_element_type=jnp.float32
    )
    up_weight_grad = jnp.einsum(
        "gech,gecd->ehd", up_grad, inputs, preferred_element_type=jnp.float32
    )
    down_weight_grad = jnp.einsum(
        "gech,gecd->ehd", hidden, scaled, preferred_element_type=jnp.float32
    )
    input_grad = jnp.einsum(
        "gech,ehd->gecd", gate_grad, weights_in[:, 0], preferred_element_type=jnp.float32
    )
    input_grad = input_grad + jnp.einsum(
        "gech,ehd->gecd", up_grad, weights_in[:, 1], preferred_element_type=jnp.float32
    )
    return (jnp.stack([gate_weight_grad, up_weight_grad], axis=1), down_weight_grad, input_grad)


def body(tokens, cotangent, routes, route_weights, capacity, w_in, w_down):
    experts = capacity.shape[0]
    expert_devs = lax.axis_size("expert")
    local_experts = experts // expert_devs
    tok_rows = tokens.shape[0]
    width = tokens.shape[1]
    slots = tok_rows * 2 // experts
    power = experts & (experts - 1) == 0 and experts % 8 == 0
    if local_experts == 1 and slots % 16 == 0 and power and lax.axis_size("dp") == 4:
        return fused(tokens, cotangent, routes, route_weights, capacity, w_in, w_down)
    flat_expert = routes.reshape(-1)
    expert_ids = jnp.arange(experts, dtype=jnp.int32)
    onehot = (flat_expert[:, None] == expert_ids[None, :]).astype(jnp.int32)
    ids = jnp.arange(flat_expert.shape[0], dtype=jnp.int32)
    before = (ids[None, :] < ids[:, None]).astype(jnp.float32)
    earlier = jnp.dot(before, onehot.astype(jnp.float32)).astype(jnp.int32)
    route_rank = jnp.sum(earlier * onehot, axis=1)
    cap_limit = jnp.sum(onehot * capacity[None, :], axis=1)
    kept_mask = route_rank < cap_limit
    dummy = experts * slots
    slot_target = jnp.where(kept_mask, flat_expert * slots + route_rank, dummy)
    route_count = 2 * tok_rows
    route_ids = jnp.arange(route_count, dtype=jnp.int32)
    slot_owner = (
        jnp.full((dummy + 1,), route_count, jnp.int32).at[slot_target].set(route_ids)[:dummy]
    )
    token_of = slot_owner // 2
    padded_tokens = jnp.concatenate([tokens, jnp.zeros((1, width), tokens.dtype)], axis=0)
    padded_cot = jnp.concatenate([cotangent, jnp.zeros((1, width), cotangent.dtype)], axis=0)
    padded_weights = jnp.concatenate(
        [route_weights.reshape(-1), jnp.zeros((1,), jnp.float32)], axis=0
    )
    bucket_shape = (expert_devs, local_experts, slots, width)
    send_inputs = padded_tokens[token_of].reshape(bucket_shape)
    send_scaled = (
        (padded_weights[slot_owner][:, None] * padded_cot[token_of].astype(jnp.float32))
        .astype(jnp.bfloat16)
        .reshape(bucket_shape)
    )
    recv_inputs = lax.all_to_all(send_inputs, "expert", split_axis=0, concat_axis=0, tiled=True)
    use_inputs = lax.all_gather(recv_inputs, "dp", axis=0, tiled=True)
    saved, partial_out = expert_forward(use_inputs, w_in, w_down)
    out_local = lax.psum_scatter(
        partial_out.astype(jnp.bfloat16), "dp", scatter_dimension=0, tiled=True
    )
    out_back = lax.all_to_all(out_local, "expert", split_axis=0, concat_axis=0, tiled=True)
    recv_scaled = lax.all_to_all(send_scaled, "expert", split_axis=0, concat_axis=0, tiled=True)
    use_scaled = lax.all_gather(recv_scaled, "dp", axis=0, tiled=True)
    in_weight_grad, down_weight_grad, input_grad = expert_backward(
        use_inputs, use_scaled, w_in, w_down, saved
    )
    grad_local = lax.psum_scatter(
        input_grad.astype(jnp.bfloat16), "dp", scatter_dimension=0, tiled=True
    )
    grad_back = lax.all_to_all(grad_local, "expert", split_axis=0, concat_axis=0, tiled=True)
    flat_out = jnp.concatenate(
        [out_back.reshape(dummy, width), jnp.zeros((1, width), jnp.bfloat16)], axis=0
    )
    flat_grad = jnp.concatenate(
        [grad_back.reshape(dummy, width), jnp.zeros((1, width), jnp.bfloat16)], axis=0
    )
    out_route = flat_out[slot_target].reshape(tok_rows, 2, width).astype(jnp.float32)
    grad_route = flat_grad[slot_target].reshape(tok_rows, 2, width).astype(jnp.float32)
    mixed = jnp.sum(route_weights[:, :, None] * out_route, axis=1).astype(jnp.bfloat16)
    d_route_weights = jnp.sum(out_route * cotangent.astype(jnp.float32)[:, None, :], axis=2)
    d_tokens = jnp.sum(grad_route, axis=1).astype(jnp.bfloat16)
    return (
        mixed,
        d_tokens,
        d_route_weights,
        in_weight_grad.astype(jnp.bfloat16),
        down_weight_grad.astype(jnp.bfloat16),
    )


def solution(mesh):
    placed = (
        P(("dp", "expert"), None),
        P(("dp", "expert"), None),
        P(("dp", "expert"), None),
        P(("dp", "expert"), None),
        P(),
        P("expert", None, "dp", None),
        P("expert", "dp", None),
    )
    return jax.shard_map(
        body,
        mesh=mesh,
        in_specs=placed,
        out_specs=(
            P(("dp", "expert"), None),
            P(("dp", "expert"), None),
            P(("dp", "expert"), None),
            P("expert", None, "dp", None),
            P("expert", "dp", None),
        ),
        check_vma=False,
    )
```
